512 devices in a mesh: dp: 64 (over z_lo, y, core), mp: 8 (over z_hi, x).
Axes of the slice: x: 4, y: 8, z: 8 (z_hi: 2, z_lo: 4; z = z_hi * 4 + z_lo), core: 2. Of those that a mesh axis runs over, the one named last changes fastest.
Arguments:
- inputs: bfloat16 [30720, 192], P('dp'), may hold values from -80 to 80
- cotangent: bfloat16 [30720, 36864], P('dp', 'mp'), may hold values from -80 to 80
- matrix: float32 [192, 36864], P('dp', 'mp'), may hold values from -60 to 60
- momentum: float32 [192, 36864], P('dp', 'mp'), may hold values from -0.4375 to 0.4375
- row_factor: float32 [192], P('dp'), as said below
- col_factor: float32 [36864], P('mp'), may hold values from 0.010368 to 30.72
- row_rest: float32 [192], P('dp'), may hold values from 36864 to 14745600
- col_rest: float32 [36864], P('mp'), may hold values from 192 to 576000
Outputs:
- new_matrix: float32 [192, 36864], P('dp', 'mp')
- new_momentum: float32 [192, 36864], P('dp', 'mp')
- new_row: float32 [192], P('dp')
- new_col: float32 [36864], P('mp')
The draws below stay inside these ranges and needn't reach their ends.
Inputs may be any that keep to these rules, and one draw needn't show every extreme that they name: `row_factor`: each entry is positive.
All inputs are finite; a program needn't handle non-finite values.
Results may differ from the reference program's by a relative error of at most 0.0003.
Values sent between devices are 32-bit elements; how exact they have to be, the bound alone decides.
A program may use at most 64 MiB of HBM per device.

```python
import math
import jax
import jax.numpy as jnp
from jax import lax

FULL_ROWS = 18432
FULL_COLS = 73728
C = 36864
ROWS = 192
TOKENS = 30720


def draw_inputs(key, part):
    key = jax.random.fold_in(key, 11)
    first, second = jax.random.split(key, 2)
    position = jnp.arange(ROWS, dtype=jnp.float32) / ROWS
    scales = 3.0 ** position * jnp.exp(jax.random.uniform(second, (ROWS,), jnp.float32, 0.0, 1.3862944))
    base = jnp.clip(jax.random.normal(first, (TOKENS, ROWS), jnp.float32), -5.0, 5.0)
    return (base * scales[None, :]).astype(jnp.bfloat16)


def draw_cotangent(key, part):
    key = jax.random.fold_in(key, 23)
    first, second = jax.random.split(key, 2)
    position = jnp.arange(C, dtype=jnp.float32) / C
    scales = 3.0 ** position * jnp.exp(jax.random.uniform(second, (C,), jnp.float32, 0.0, 1.3862944))
    scales = scales * TOKENS ** (-0.5)
    base = jnp.clip(jax.random.normal(first, (TOKENS, C), jnp.float32), -5.0, 5.0)
    return (base * scales[None, :]).astype(jnp.bfloat16)


def draw_matrix(key, part):
    key = jax.random.fold_in(key, 41)
    row_pos = jnp.arange(ROWS, dtype=jnp.float32) / ROWS
    col_pos = jnp.arange(C, dtype=jnp.float32) / C
    base = jnp.clip(jax.random.normal(key, (ROWS, C), jnp.float32), -5.0, 5.0)
    scales = 1.5 * (2.5 ** row_pos)[:, None] * (2.5 ** col_pos)[None, :]
    return base * scales


def draw_row_factor(key, part):
    key = jax.random.fold_in(key, 53)
    position = jnp.arange(ROWS, dtype=jnp.float32) / ROWS
    jitter = jnp.exp(jax.random.uniform(key, (ROWS,), jnp.float32, 0.0, 0.6931472))
    trend = 100.0 ** position
    return float(C) / float(FULL_COLS) * 20.0 * trend * jitter


def steps_of(stream_key, dims, cuts, low, largest):
    def one(dim, shards_of):
        heights = jax.random.uniform(jax.random.fold_in(jax.random.fold_in(stream_key, 6), dim), (shards_of,), jnp.float32, low / len(cuts), largest / len(cuts))
        return jnp.repeat(jnp.exp(heights), dims[dim] // shards_of).reshape((-1,) + (1,) * (len(dims) - dim - 1))

    factor_of = one(*cuts[0])
    for cut in cuts[1:]:
        factor_of = factor_of * one(*cut)
    return factor_of


def gaussian(key, extent, scale, reach, pieces=(), held_as=jnp.bfloat16):
    drawn = scale * jax.random.normal(key, extent, jnp.float32)
    if pieces:
        drawn = drawn * steps_of(key, extent, pieces, -0.22, 0.18)
    return jnp.clip(drawn, -reach, reach).astype(held_as)


def setup_inputs(seed: int = 0) -> dict:
    streams_of = jax.random.split(jax.random.key(seed), 9)
    inputs = draw_inputs(jax.random.fold_in(streams_of[8], 71), 0)
    cotangent = draw_cotangent(jax.random.fold_in(streams_of[8], 71), 0)
    matrix = draw_matrix(jax.random.fold_in(streams_of[8], 71), 0)
    momentum = gaussian(streams_of[3], (ROWS, C), 0.03, 0.4375, ((0, 64), (1, 8)), jnp.float32)
    row_factor = draw_row_factor(jax.random.fold_in(streams_of[8], 71), 0)
    col_factor = jnp.clip(jnp.exp(math.log(30.72) - 7.993945 * jax.random.uniform(streams_of[5], (C,), jnp.float32) ** steps_of(streams_of[5], (C,), ((0, 8),), -0.2, 0.2)), 0.010368, 30.72)
    row_rest = jnp.clip(jnp.exp(math.log(14745600) - 5.9914645 * jax.random.uniform(streams_of[6], (ROWS,), jnp.float32) ** steps_of(streams_of[6], (ROWS,), ((0, 64),), -0.2, 0.2)), 36864.0, 14745600)
    col_rest = jnp.clip(jnp.exp(math.log(576000.0) - 8.006368 * jax.random.uniform(streams_of[7], (C,), jnp.float32) ** steps_of(streams_of[7], (C,), ((0, 8),), -0.2, 0.2)), 192.0, 576000.0)
    return {"inputs": inputs, "cotangent": cotangent, "matrix": matrix, "momentum": momentum, "row_factor": row_factor, "col_factor": col_factor, "row_rest": row_rest, "col_rest": col_rest}


beta_two = 1.0 - 10.0 ** (-0.8)
beta_one = 0.9
rel_step = 0.01
eps_sq = 1e-30

def reference(inputs, cotangent, matrix, momentum, row_factor, col_factor, row_rest, col_rest):
    entries = float(ROWS) * float(C)
    gradient = lax.dot_general(inputs, cotangent, (((0,), (0,)), ((), ())), preferred_element_type=jnp.float32)
    squares = gradient * gradient + eps_sq
    new_row = beta_two * row_factor + (1.0 - beta_two) * ((lax.optimization_barrier(jnp.sum(squares, axis=1)) + row_rest) / FULL_COLS)
    new_col = beta_two * col_factor + (1.0 - beta_two) * ((lax.optimization_barrier(jnp.sum(squares, axis=0)) + col_rest) / FULL_ROWS)
    row_mean = jnp.sum(new_row) / ROWS
    scaled = gradient * lax.rsqrt(new_row / row_mean)[:, None] * lax.rsqrt(new_col)[None, :]
    matrix_rms = jnp.sqrt(jnp.sum(matrix * matrix) / entries)
    new_momentum = beta_one * momentum + (1.0 - beta_one) * rel_step * matrix_rms * scaled
    new_matrix = matrix - new_momentum
    return (new_matrix, new_momentum, new_row, new_col)
```

```python
import functools

import jax
import jax.numpy as jnp
from jax import lax
from jax.experimental import pallas as pl
from jax.experimental.pallas import tpu as pltpu
from jax.sharding import PartitionSpec as P

FULL_ROWS = 18432
FULL_COLS = 73728
ROWS = 192
BLOCK_COLS = 36864

beta_two = 1.0 - 10.0 ** (-0.8)
beta_one = 0.9
rel_step = 0.01
eps_sq = 1e-30

MESH = pl.DeviceIdType.MESH
F32 = jnp.float32
VMEM = pltpu.VMEM

LANE_TILES = 9
TILES = 27
CHUNK = TILES * 8
GROUP = LANE_TILES * 128
SPREAD = 32
STREAMS = ((0, 0, 1, 4), (1, 0, -1, 4), (0, 1, -1, 3), (1, 1, 1, 3))
GROUP_ORDER = (0, 1, 3, 2)
GATHERED = 4 * SPREAD
SUMS = GATHERED + 4 * 16


def send(src, dst, send_sem, recv_sem, target):
    return pltpu.make_async_remote_copy(
        src_ref=src, dst_ref=dst, send_sem=send_sem, recv_sem=recv_sem, device_id=target, device_id_type=MESH
    )


def reduce_kernel(
    inputs_hbm, cot_hbm, matrix_ref, row_factor_ref, row_rest_ref, out_ref,
    inp, lhs, cot, part, sib, ring, zrecv, spread, gathered, small, small_recv, m1, p1, m2, p2,
    in_sem, cot_sem, sib_ss, sib_rs, small_ss, small_rs, ring_ss, ring_rs, z_ss, z_rs, g_ss, g_rs,
    p1_ss, p1_rs, p2_ss, p2_rs,
):
    d = lax.axis_index("dp")
    m = lax.axis_index("mp")
    z = d // 16
    y = lax.rem(d // 2, 8)
    c = lax.rem(d, 2)
    h = y // 4
    q = lax.rem(y, 4)
    home = z // 2
    active = c == home

    def dev(zz, yy, cc, mm):
        return (zz * 16 + yy * 2 + cc, mm)

    def turn(v, k, n):
        return lax.rem(v + k + n, n)

    in_copy = pltpu.make_async_copy(inputs_hbm, inp, in_sem)
    in_copy.start()
    cot_copies = []
    for n, off in enumerate(GROUP_ORDER):
        g = turn(q, off, 4)
        copy = pltpu.make_async_copy(
            cot_hbm.at[:, pl.ds(pl.multiple_of(g * GROUP, 128), GROUP)], cot.at[n], cot_sem.at[n]
        )
        copy.start()
        cot_copies.append(copy)

    barrier = pltpu.get_barrier_semaphore()

    def hello(target):
        pl.semaphore_signal(barrier, inc=1, device_id=target, device_id_type=MESH)

    hello(dev(z, y, 1 - c, m))
    for dy in range(1, 8):
        for cc in range(2):
            hello(dev(z, turn(y, dy, 8), cc, m))

    @pl.when(active)
    def _():
        for dz in range(4):
            for dm in range(8):
                if dz or dm:
                    zz = turn(z, dz, 4)
                    hello(dev(zz, y, zz // 2, turn(m, dm, 8)))
        for i in range(2):
            hello(dev((1 - home) * 2 + i, y, c, m))

    @pl.when(jnp.logical_not(active))
    def _():
        for i in range(2):
            hello(dev(2 * c + i, y, c, m))

    row = lax.broadcasted_iota(jnp.int32, (ROWS, ROWS), 0)
    col = lax.broadcasted_iota(jnp.int32, (ROWS, ROWS), 1)
    block = (row * 2731) >> 16
    inner = row - block * 24
    want = block * 24 + 3 * (inner & 7) + (inner >> 3)
    pick = jnp.where(col == want, 1.0, 0.0).astype(jnp.bfloat16)
    in_copy.wait()
    lhs[...] = jnp.dot(pick, inp[...], preferred_element_type=F32).astype(jnp.bfloat16)

    mat = matrix_ref[...]
    msq = jnp.sum(jnp.sum(mat * mat, axis=0, keepdims=True), axis=1, keepdims=True)
    base = jnp.float32(0.0)
    for j in range(3):
        base = base + beta_two * row_factor_ref[j] + (1.0 - beta_two) * (row_rest_ref[j] * (1.0 / FULL_COLS))
    sub8 = lax.broadcasted_iota(jnp.int32, (8, 128), 0)
    lane8 = lax.broadcasted_iota(jnp.int32, (8, 128), 1)
    small[...] = jnp.where(sub8 == 2, msq, jnp.where(sub8 == 3, base, 0.0))

    def product(n):
        cot_copies[n].wait()
        g = turn(q, GROUP_ORDER[n], 4)
        acc = jnp.dot(lhs[...], cot[n], preferred_element_type=F32)
        for zh in range(2):
            for i in range(2):
                for hh in range(2):
                    r0 = ((zh * 2 + i) * 2 + hh) * 24
                    for j in range(3):
                        for lb in range(LANE_TILES):
                            t = j * LANE_TILES + lb
                            part[zh, hh * 4 + g, i, t * 8 : t * 8 + 8, :] = acc[
                                r0 + j * 8 : r0 + j * 8 + 8, lb * 128 : lb * 128 + 128
                            ]

    sibling = dev(z, y, 1 - c, m)

    def sib_copy(o):
        return send(part.at[1 - c, o], sib.at[o], sib_ss.at[o], sib_rs.at[o], sibling)

    small_copy = send(small, small_recv, small_ss, small_rs, sibling)

    def pass_on(n):
        for off in (4, 0):
            sib_copy(turn(y, GROUP_ORDER[n] + off, 8)).start()

    arrived = set()

    def arrive(k):
        k %= 8
        if k not in arrived:
            arrived.add(k)
            sib_copy(turn(y, k, 8)).wait_recv()

    def ring_copy(stream, s):
        i, kind, way, n = stream
        o = turn(y, (way * (n + 1 - s)) % 8, 8)
        return send(
            part.at[c, o, i],
            ring.at[i, kind, s - 1],
            ring_ss.at[i, kind, s - 1],
            ring_rs.at[i, kind, s - 1],
            dev(z, turn(y, way % 8, 8), c, m),
        )

    def ring_step(stream, s):
        i, kind, way, n = stream
        off = (way * (n + 1 - s)) % 8
        o = turn(y, off, 8)
        arrive(off)
        total = part[c, o, i] + sib[o, i]
        if s > 1:
            ring_copy(stream, s - 1).wait_recv()
            total = total + ring[i, kind, s - 2]
        part[c, o, i] = total
        ring_copy(stream, s).start()

    product(0)
    pl.semaphore_wait(barrier, jnp.where(active, 48, 17))
    pass_on(0)
    small_copy.start()
    product(1)
    pass_on(1)
    ring_step(STREAMS[0], 1)
    ring_step(STREAMS[1], 1)
    product(2)
    pass_on(2)
    ring_step(STREAMS[2], 1)
    product(3)
    pass_on(3)
    ring_step(STREAMS[3], 1)
    for s in range(2, 5):
        for stream in STREAMS:
            if s <= stream[3]:
                ring_step(stream, s)

    arrive(0)

    def z_copy(i):
        return send(part.at[c, y, i], zrecv.at[z], z_ss.at[i], z_rs.at[z], dev(2 * c + i, y, c, m))

    for i in range(2):
        ring_copy(STREAMS[i], 4).wait_recv()
        ring_copy(STREAMS[2 + i], 3).wait_recv()
        total = part[c, y, i] + sib[y, i] + ring[i, 0, 3] + ring[i, 1, 2]

        @pl.when(z != 2 * c + i)
        def _():
            part[c, y, i] = total
            z_copy(i).start()

        @pl.when(z == 2 * c + i)
        def _():
            zrecv[z] = total

    small_copy.wait_recv()

    def first_copy(dz, dm):
        zz = turn(z, dz, 4)
        mm = turn(m, dm, 8)
        rows = pl.ds(0, 16) if dm == 0 else pl.ds(8, 8)
        n = dz * 8 + dm
        slot = z * 8 + m
        return send(
            m1.at[rows], p1.at[slot, rows], p1_ss.at[n], p1_rs.at[slot], dev(zz, y, zz // 2, mm)
        )

    def first_wait(dz, dm):
        zz = turn(z, dz, 4)
        mm = turn(m, dm, 8)
        rows = pl.ds(0, 16) if dm == 0 else pl.ds(8, 8)
        slot = zz * 8 + mm
        send(m1.at[rows], p1.at[slot, rows], p1_ss.at[dz * 8 + dm], p1_rs.at[slot], dev(zz, y, zz // 2, mm)).wait_recv()

    def gather_copy(dk):
        k = turn(2 * q + c, dk, 8)
        return send(
            spread.at[pl.ds(pl.multiple_of(k * SPREAD, SPREAD), SPREAD)],
            gathered.at[q],
            g_ss.at[dk],
            g_rs.at[q],
            dev(z, 4 * h + k // 2, lax.rem(k, 2), m),
        )

    def second_copy(dy, cc):
        return send(
            m2, p2.at[y], p2_ss.at[dy * 2 + cc], p2_rs.at[y],
            dev(z, turn(y, dy, 8), lax.rem(c + cc, 2), m),
        )

    first_order = [(dz, dm) for dm in (6, 5, 7, 2, 4, 1, 3, 0) for dz in (2, 1, 3, 0) if dz or dm]
    second_order = [(dy, cc) for dy in (4, 3, 5, 2, 6, 1, 7, 0) for cc in (0, 1) if dy or cc]

    @pl.when(active)
    def _():
        for dz in range(1, 4):
            zz = turn(z, dz, 4)
            send(part.at[c, y, 0], zrecv.at[zz], z_ss.at[0], z_rs.at[zz], dev(zz, y, c, m)).wait_recv()
        column = [None] * LANE_TILES
        rows = [None] * 3
        for j in range(3):
            for lb in range(LANE_TILES):
                t = j * LANE_TILES + lb
                at = slice(t * 8, t * 8 + 8)
                g = (zrecv[0, at] + zrecv[1, at]) + (zrecv[2, at] + zrecv[3, at])
                spread[pl.ds(t, 8, stride=SPREAD), :] = g
                square = g * g + eps_sq
                column[lb] = square if j == 0 else column[lb] + square
                rows[j] = square if lb == 0 else rows[j] + square
        for lb in range(LANE_TILES):
            m1[lb : lb + 1, :] = jnp.sum(column[lb], axis=0, keepdims=True)
        every = jnp.sum(rows[0] + rows[1] + rows[2], axis=0, keepdims=True)
        m1[9:10, :] = jnp.broadcast_to(jnp.sum(every, axis=1, keepdims=True), (1, 128))
        m1[10:12, :] = small[2:4, :] + small_recv[2:4, :]
        for j in range(3):
            each = jnp.broadcast_to(jnp.sum(rows[j], axis=1, keepdims=True), (8, 128))
            m1[12 + j : 13 + j, :] = jnp.sum(jnp.where(lane8 == sub8, each, 0.0), axis=0, keepdims=True)
        m1[15:16, :] = jnp.zeros((1, 128), F32)
        for dz, dm in first_order:
            first_copy(dz, dm).start()
        for dk in range(1, 8):
            gather_copy(dk).start()
        gathered[q] = spread[pl.ds(pl.multiple_of((2 * q + c) * SPREAD, SPREAD), SPREAD), :]
        own = m1[8:16, :]
        same_m, same_z, other = own, own, jnp.zeros((8, 128), F32)
        same_m_top = m1[0:8, :]
        for dz, dm in reversed(first_order):
            first_wait(dz, dm)
            slot = turn(z, dz, 4) * 8 + turn(m, dm, 8)
            tile = p1[slot, 8:16, :]
            if dm == 0:
                same_m = same_m + tile
                same_m_top = same_m_top + p1[slot, 0:8, :]
            elif dz == 0:
                same_z = same_z + tile
            else:
                other = other + tile
        everyone = same_m + same_z - own + other
        m2[0:8, :] = same_m_top
        m2[8:16, :] = jnp.where(sub8 == 0, same_m, jnp.where(sub8 < 4, everyone, same_z))
        for dy, cc in second_order:
            second_copy(dy, cc).start()
        p2[y] = m2[...]

    for dy in range(8):
        yy = turn(y, dy, 8)
        landed = send(m2, p2.at[yy], p2_ss.at[0], p2_rs.at[yy], dev(z, yy, 1 - c, m))
        if dy == 0:

            @pl.when(jnp.logical_not(active))
            def _():
                landed.wait_recv()
        else:
            landed.wait_recv()
    for dq in range(4):
        qq = turn(q, dq, 4)
        landed = send(
            spread.at[pl.ds(0, SPREAD)], gathered.at[qq], g_ss.at[0], g_rs.at[qq], dev(z, 4 * h + qq, 1 - c, m)
        )
        if dq == 0:

            @pl.when(jnp.logical_not(active))
            def _():
                landed.wait_recv()
        else:
            landed.wait_recv()

    for qq in range(4):
        out_ref[qq * SPREAD : (qq + 1) * SPREAD, :] = gathered[qq]
        out_ref[GATHERED + qq * 16 : GATHERED + qq * 16 + 16, :] = p2[qq] + p2[4 + qq]
    all_y = p2[0, 8:16, :]
    for yy in range(1, 8):
        all_y = all_y + p2[yy, 8:16, :]
    same_h = p2[4 * h, 8:16, :]
    for qq in range(1, 4):
        same_h = same_h + p2[4 * h + qq, 8:16, :]
    mine = jnp.sum(jnp.where(lane8 == 2 * q + c, same_h, 0.0), axis=1, keepdims=True)
    out_ref[SUMS : SUMS + 8, :] = jnp.where(sub8 < 4, all_y, jnp.broadcast_to(mine, (8, 128)))

    for o in range(8):
        sib_copy(o).wait_send()
    small_copy.wait_send()
    for stream in STREAMS:
        for s in range(1, stream[3] + 1):
            ring_copy(stream, s).wait_send()
    for i in range(2):

        @pl.when(z != 2 * c + i)
        def _():
            z_copy(i).wait_send()

    @pl.when(active)
    def _():
        for dz, dm in first_order:
            first_copy(dz, dm).wait_send()
        for dk in range(1, 8):
            gather_copy(dk).wait_send()
        for dy, cc in second_order:
            second_copy(dy, cc).wait_send()


def finish_kernel(
    sums_ref, matrix_ref, momentum_ref, row_factor_ref, row_rest_ref, col_factor_ref, col_rest_ref,
    new_matrix_ref, new_momentum_ref, new_row_ref, new_col_ref,
):
    entries = float(ROWS) * float(BLOCK_COLS)
    total = sums_ref[SUMS + 1 : SUMS + 2, :]
    matrix_sq = sums_ref[SUMS + 2 : SUMS + 3, :]
    base = sums_ref[SUMS + 3 : SUMS + 4, :] * 0.125
    row_mean = (base + (1.0 - beta_two) * (total / FULL_COLS)) / ROWS
    step = (1.0 - beta_one) * rel_step * jnp.sqrt(matrix_sq / entries)
    row_sums = sums_ref[SUMS + 4 : SUMS + 7, :]
    sub = lax.broadcasted_iota(jnp.int32, (3, 128), 0)

    def down(ref):
        return jnp.where(sub == 0, ref[0], jnp.where(sub == 1, ref[1], ref[2]))

    new_row = beta_two * down(row_factor_ref) + (1.0 - beta_two) * ((row_sums + down(row_rest_ref)) / FULL_COLS)
    for j in range(3):
        new_row_ref[j] = new_row[j, 0]
    row_scale = lax.rsqrt(new_row / row_mean) * step
    for qq in range(4):
        at = slice(qq * LANE_TILES, (qq + 1) * LANE_TILES)
        column_sum = sums_ref[GATHERED + qq * 16 : GATHERED + qq * 16 + LANE_TILES, :]
        new_col = beta_two * col_factor_ref[at, :] + (1.0 - beta_two) * (
            (column_sum + col_rest_ref[at, :]) / FULL_ROWS
        )
        new_col_ref[at, :] = new_col
        inverse_col = lax.rsqrt(new_col)
        for lb in range(LANE_TILES):
            b = (qq * LANE_TILES + lb) * 128
            g = sums_ref[pl.ds(qq * SPREAD + lb, 3, stride=LANE_TILES), :]
            change = g * row_scale * inverse_col[lb : lb + 1, :]
            new_momentum = beta_one * momentum_ref[:, b : b + 128] + change
            new_momentum_ref[:, b : b + 128] = new_momentum
            new_matrix_ref[:, b : b + 128] = matrix_ref[:, b : b + 128] - new_momentum


def on_device(inputs, cotangent, matrix, momentum, row_factor, col_factor, row_rest, col_rest):
    vmem = pl.BlockSpec(memory_space=VMEM)
    smem = pl.BlockSpec(memory_space=pltpu.SMEM)
    hbm = pl.BlockSpec(memory_space=pl.ANY)
    dma = pltpu.SemaphoreType.DMA
    sums = pl.pallas_call(
        reduce_kernel,
        out_shape=jax.ShapeDtypeStruct((SUMS + 8, 128), F32),
        in_specs=[hbm, hbm, vmem, smem, smem],
        out_specs=vmem,
        scratch_shapes=[
            VMEM((ROWS, 480), jnp.bfloat16),
            VMEM((ROWS, 480), jnp.bfloat16),
            VMEM((4, 480, GROUP), jnp.bfloat16),
            VMEM((2, 8, 2, CHUNK, 128), F32),
            VMEM((8, 2, CHUNK, 128), F32),
            VMEM((2, 2, 4, CHUNK, 128), F32),
            VMEM((4, CHUNK, 128), F32),
            VMEM((8 * SPREAD, 128), F32),
            VMEM((4, SPREAD, 128), F32),
            VMEM((8, 128), F32),
            VMEM((8, 128), F32),
            VMEM((16, 128), F32),
            VMEM((32, 16, 128), F32),
            VMEM((16, 128), F32),
            VMEM((8, 16, 128), F32),
            dma, dma((4,)), dma((8,)), dma((8,)), dma, dma,
            dma((2, 2, 4)), dma((2, 2, 4)), dma((2,)), dma((4,)), dma((8,)), dma((4,)),
            dma((32,)), dma((32,)), dma((16,)), dma((8,)),
        ],
        compiler_params=pltpu.CompilerParams(
            collective_id=0, has_side_effects=True, vmem_limit_bytes=40 * 1024 * 1024
        ),
        name="reduce",
    )(inputs.T, cotangent, matrix, row_factor, row_rest)
    new_matrix, new_momentum, new_row, new_col = pl.pallas_call(
        finish_kernel,
        out_shape=(
            jax.ShapeDtypeStruct(matrix.shape, F32),
            jax.ShapeDtypeStruct(matrix.shape, F32),
            jax.ShapeDtypeStruct((3,), F32),
            jax.ShapeDtypeStruct((36, 128), F32),
        ),
        in_specs=[vmem, vmem, vmem, smem, smem, vmem, vmem],
        out_specs=(vmem, vmem, smem, vmem),
        name="finish",
    )(sums, matrix, momentum, row_factor, row_rest, col_factor.reshape(36, 128), col_rest.reshape(36, 128))
    return (new_matrix, new_momentum, new_row, new_col.reshape(4608))


def solution(mesh):
    placed = (
        P("dp", None),
        P("dp", "mp"),
        P("dp", "mp"),
        P("dp", "mp"),
        P("dp"),
        P("mp"),
        P("dp"),
        P("mp"),
    )
    return jax.shard_map(
        on_device,
        mesh=mesh,
        in_specs=placed,
        out_specs=(P("dp", "mp"), P("dp", "mp"), P("dp"), P("mp")),
        check_vma=False,
    )
```

```python
import functools

import jax
import jax.numpy as jnp
from jax import lax
from jax.experimental import pallas as pl
from jax.experimental.pallas import tpu as pltpu
from jax.sharding import PartitionSpec as P

FULL_ROWS = 18432
FULL_COLS = 73728
ROWS = 192
BLOCK_COLS = 36864

beta_two = 1.0 - 10.0 ** (-0.8)
beta_one = 0.9
rel_step = 0.01
eps_sq = 1e-30

MESH = pl.DeviceIdType.MESH
F32 = jnp.float32
VMEM = pltpu.VMEM

LANE_TILES = 9
A_LANES = 6
A_ROWS = A_LANES * 24
B_ROWS = (LANE_TILES - A_LANES) * 24
GROUP = LANE_TILES * 128
SPREAD = 32
STREAMS = ((0, 0, 1, 4), (1, 0, -1, 4), (0, 1, -1, 3), (1, 1, 1, 3))
GROUP_ORDER = (0, 1, 3, 2)
GATHERED = 4 * SPREAD
SUMS = GATHERED + 4 * 16
FIRST_ORDER = tuple((dz, dm) for dm in (6, 5, 7, 2, 4, 1, 3, 0) for dz in (2, 1, 3, 0) if dz or dm)
SECOND_ORDER = tuple((dy, cc) for dy in (4, 3, 5, 2, 6, 1, 7, 0) for cc in (0, 1) if dy or cc)

GATHER_ORDER = ((2, 0), (2, 1), (1, 0), (1, 1), (3, 0), (3, 1), (0, 1))
Y_AT = 5


def slot_of(dz, dm):
    if dm == 0:
        return pl.ds((dz - 1) * 16, 16)
    return pl.ds(48 + (dz * 7 + dm - 1) * 8, 8)


def send(src, dst, send_sem, recv_sem, target):
    return pltpu.make_async_remote_copy(
        src_ref=src, dst_ref=dst, send_sem=send_sem, recv_sem=recv_sem, device_id=target, device_id_type=MESH
    )


def landed(ref, sem):
    pltpu.make_async_copy(ref, ref, sem).wait()


def reduce_kernel(
    inputs_hbm, cot_hbm, matrix_hbm, row_factor_hbm, row_rest_hbm, out_ref,
    inp, matrix_ref, row_factor_ref, row_rest_ref, lhs, cot, part, sib, qpart, qsib, ring, zrecv, zq, yq,
    spread, gathered, small, small_recv, m1, p1, m2, p2,
    in_sem, late_sem, cot_sem, sib_ss, sib_rs, qsib_ss, qsib_rs, small_ss, small_rs, ring_ss, ring_rs,
    z_ss, z_rs, zq_ss, zq_rs, yq_ss, yq_rs, g_ss, g_rs, g_own, p1_ss, p1_rs, p2_ss, p2_rs, p2_own,
):
    d = lax.axis_index("dp")
    m = lax.axis_index("mp")
    z = d // 16
    y = lax.rem(d // 2, 8)
    c = lax.rem(d, 2)
    h = y // 4
    q = lax.rem(y, 4)
    home = z // 2
    active = c == home

    def dev(zz, yy, cc, mm):
        return (zz * 16 + yy * 2 + cc, mm)

    def turn(v, k, n):
        return lax.rem(v + k + n, n)

    in_copy = pltpu.make_async_copy(inputs_hbm, inp, in_sem)
    in_copy.start()
    late_copies = []
    for n, (src, dst) in enumerate(
        ((matrix_hbm, matrix_ref), (row_factor_hbm, row_factor_ref), (row_rest_hbm, row_rest_ref))
    ):
        late_copies.append(pltpu.make_async_copy(src, dst, late_sem.at[n]))
    cot_copies = []
    for n, off in enumerate(GROUP_ORDER):
        g = turn(q, off, 4)
        copy = pltpu.make_async_copy(
            cot_hbm.at[:, pl.ds(pl.multiple_of(g * GROUP, 128), GROUP)], cot.at[n], cot_sem.at[n]
        )
        cot_copies.append(copy)
    cot_copies[0].start()

    barrier = pltpu.get_barrier_semaphore()

    def hello(target):
        pl.semaphore_signal(barrier, inc=1, device_id=target, device_id_type=MESH)

    @pl.when(active)
    def _():
        for dz, dm in FIRST_ORDER:
            zz = turn(z, dz, 4)
            hello(dev(zz, y, zz // 2, turn(m, dm, 8)))
        for i in range(2):
            hello(dev((1 - home) * 2 + i, y, c, m))

    @pl.when(jnp.logical_not(active))
    def _():
        for i in range(2):
            hello(dev(2 * c + i, y, c, m))

    for dy, cc in SECOND_ORDER:
        hello(dev(z, turn(y, dy, 8), lax.rem(c + cc, 2), m))

    row = lax.broadcasted_iota(jnp.int32, (ROWS, ROWS), 0)
    col = lax.broadcasted_iota(jnp.int32, (ROWS, ROWS), 1)
    block = (row * 2731) >> 16
    inner = row - block * 24
    want = block * 24 + 3 * (inner & 7) + (inner >> 3)
    pick = jnp.where(col == want, 1.0, 0.0).astype(jnp.bfloat16)
    in_copy.wait()
    cot_copies[1].start()
    lhs[...] = jnp.dot(pick, inp[...], preferred_element_type=F32).astype(jnp.bfloat16)

    sub8 = lax.broadcasted_iota(jnp.int32, (8, 128), 0)
    lane8 = lax.broadcasted_iota(jnp.int32, (8, 128), 1)

    def product(n):
        cot_copies[n].wait()
        if n < 2:
            cot_copies[n + 2].start()
        if n == 2:
            for copy in late_copies:
                copy.start()
        g = turn(q, GROUP_ORDER[n], 4)
        acc = jnp.dot(lhs[...], cot[n], preferred_element_type=F32)
        for zh in range(2):
            for i in range(2):
                for hh in range(2):
                    r0 = ((zh * 2 + i) * 2 + hh) * 24
                    for lb in range(LANE_TILES):
                        for j in range(3):
                            tile = acc[r0 + j * 8 : r0 + j * 8 + 8, lb * 128 : lb * 128 + 128]
                            if lb < A_LANES:
                                t = (lb * 3 + j) * 8
                                part[zh, hh * 4 + g, i, t : t + 8, :] = tile
                            else:
                                t = ((lb - A_LANES) * 3 + j) * 8
                                qpart[zh, g, i, hh, t : t + 8, :] = tile

    sibling = dev(z, y, 1 - c, m)

    def sib_copy(o):
        return send(part.at[1 - c, o], sib.at[o], sib_ss, sib_rs.at[o], sibling)

    def qsib_copy(g):
        return send(qpart.at[1 - c, g], qsib.at[g], qsib_ss, qsib_rs.at[g], sibling)

    small_copy = send(small, small_recv, small_ss, small_rs, sibling)

    def pass_on(n):
        for off in (4, 0):
            sib_copy(turn(y, GROUP_ORDER[n] + off, 8)).start()
        qsib_copy(turn(q, GROUP_ORDER[n], 4)).start()

    def zq_copy(g, i):
        return send(qpart.at[c, g, i], zq.at[z, g], zq_ss.at[i], zq_rs, dev(2 * c + i, y, c, m))

    def along_z(n):
        g = turn(q, GROUP_ORDER[n], 4)
        qsib_copy(g).wait_recv()
        for i in range(2):
            qpart[c, g, i] = qpart[c, g, i] + qsib[g, i]

            @pl.when(z != 2 * c + i)
            def _():
                zq_copy(g, i).start()

    arrived = set()

    def arrive(k):
        k %= 8
        if k not in arrived:
            arrived.add(k)
            sib_copy(turn(y, k, 8)).wait_recv()

    def ring_copy(stream, s):
        i, kind, way, n = stream
        o = turn(y, (way * (n + 1 - s)) % 8, 8)
        return send(
            part.at[c, o, i],
            ring.at[(i * 2 + kind) * 4 + s - 1],
            ring_ss,
            ring_rs.at[i, kind, s - 1],
            dev(z, turn(y, way % 8, 8), c, m),
        )

    def ring_step(stream, s):
        i, kind, way, n = stream
        off = (way * (n + 1 - s)) % 8
        o = turn(y, off, 8)
        arrive(off)
        total = part[c, o, i] + sib[o, i]
        if s > 1:
            ring_copy(stream, s - 1).wait_recv()
            total = total + ring[(i * 2 + kind) * 4 + s - 2]
        part[c, o, i] = total
        ring_copy(stream, s).start()

    product(0)
    pl.semaphore_wait(barrier, jnp.where(active, 48, 17))
    pass_on(0)
    product(1)
    pass_on(1)
    ring_step(STREAMS[0], 1)
    ring_step(STREAMS[1], 1)
    product(2)
    pass_on(2)
    ring_step(STREAMS[2], 1)
    along_z(0)
    product(3)
    pass_on(3)
    ring_step(STREAMS[3], 1)
    for n in (1, 2, 3):
        along_z(n)

    for copy in late_copies:
        copy.wait()
    mat = matrix_ref[...]
    msq = jnp.sum(jnp.sum(mat * mat, axis=0, keepdims=True), axis=1, keepdims=True)
    base = jnp.float32(0.0)
    for j in range(3):
        base = base + beta_two * row_factor_ref[j] + (1.0 - beta_two) * (row_rest_ref[j] * (1.0 / FULL_COLS))
    small[...] = jnp.where(sub8 == 2, msq, jnp.where(sub8 == 3, base, 0.0))

    small_copy.start()

    def yq_copy(g, hh):
        return send(
            qpart.at[c, g, z - 2 * home, hh], yq.at[y], yq_ss, yq_rs, dev(z, 4 * hh + g, c, m)
        )

    def along_y():
        @pl.when(active)
        def _():
            landed(zq.at[pl.ds(0, 3)], zq_rs)
            for dy in (4, 3, 5, 2, 6, 1, 7, 0):
                yy = turn(y, dy, 8)
                g, hh = lax.rem(yy, 4), yy // 4
                total = qpart[c, g, z - 2 * home, hh]
                for dz in range(1, 4):
                    total = total + zq[turn(z, dz, 4), g, hh]
                if dy:
                    qpart[c, g, z - 2 * home, hh] = total
                    yq_copy(g, hh).start()
                else:
                    yq[y] = total

    for s in range(2, 5):
        if s == Y_AT:
            along_y()
        for stream in STREAMS:
            if s <= stream[3]:
                ring_step(stream, s)
    if Y_AT > 4:
        along_y()

    arrive(0)

    def z_copy(i):
        return send(part.at[c, y, i], zrecv.at[z], z_ss.at[i], z_rs, dev(2 * c + i, y, c, m))

    for i in range(2):
        ring_copy(STREAMS[2 + i], 3).wait_recv()
        ring_copy(STREAMS[i], 4).wait_recv()
        total = part[c, y, i] + sib[y, i] + ring[i * 8 + 3] + ring[i * 8 + 6]

        @pl.when(z != 2 * c + i)
        def _():
            part[c, y, i] = total
            z_copy(i).start()

        @pl.when(z == 2 * c + i)
        def _():
            zrecv[z] = total

    small_copy.wait_recv()

    def first_copy(dz, dm):
        zz = turn(z, dz, 4)
        rows = pl.ds(0, 16) if dm == 0 else pl.ds(8, 8)
        slot = slot_of((4 - dz) % 4, (8 - dm) % 8)
        return send(m1.at[rows], p1.at[slot], p1_ss, p1_rs, dev(zz, y, zz // 2, turn(m, dm, 8)))

    def gather_copy(dq, cc):
        k = 2 * turn(q, dq, 4) + lax.rem(c + cc, 2)
        return send(
            spread.at[pl.ds(pl.multiple_of(k * SPREAD, SPREAD), SPREAD)],
            gathered.at[q],
            g_ss,
            g_rs if dq else g_own,
            dev(z, 4 * h + turn(q, dq, 4), lax.rem(c + cc, 2), m),
        )

    def second_copy(dy, cc):
        return send(
            m2, p2.at[y], p2_ss, p2_rs if dy else p2_own, dev(z, turn(y, dy, 8), lax.rem(c + cc, 2), m)
        )

    @pl.when(active)
    def _():
        landed(yq.at[pl.ds(0, 7)], yq_rs)
        landed(zrecv.at[pl.ds(0, 3)], z_rs)
        column = [None] * LANE_TILES
        rows = [None] * 3
        for lb in range(LANE_TILES):
            for j in range(3):
                if lb < A_LANES:
                    t = (lb * 3 + j) * 8
                    at = slice(t, t + 8)
                    g = (zrecv[0, at] + zrecv[1, at]) + (zrecv[2, at] + zrecv[3, at])
                else:
                    t = ((lb - A_LANES) * 3 + j) * 8
                    at = slice(t, t + 8)
                    g = ((yq[0, at] + yq[1, at]) + (yq[2, at] + yq[3, at])) + (
                        (yq[4, at] + yq[5, at]) + (yq[6, at] + yq[7, at])
                    )
                spread[pl.ds(j * LANE_TILES + lb, 8, stride=SPREAD), :] = g
                square = g * g + eps_sq
                column[lb] = square if j == 0 else column[lb] + square
                rows[j] = square if lb == 0 else rows[j] + square
        for lb in range(LANE_TILES):
            m1[lb : lb + 1, :] = jnp.sum(column[lb], axis=0, keepdims=True)
        every = jnp.sum(rows[0] + rows[1] + rows[2], axis=0, keepdims=True)
        m1[9:10, :] = jnp.broadcast_to(jnp.sum(every, axis=1, keepdims=True), (1, 128))
        m1[10:12, :] = small[2:4, :] + small_recv[2:4, :]
        for j in range(3):
            each = jnp.broadcast_to(jnp.sum(rows[j], axis=1, keepdims=True), (8, 128))
            m1[12 + j : 13 + j, :] = jnp.sum(jnp.where(lane8 == sub8, each, 0.0), axis=0, keepdims=True)
        m1[15:16, :] = jnp.zeros((1, 128), F32)
        for dz, dm in FIRST_ORDER:
            first_copy(dz, dm).start()
        for dq, cc in GATHER_ORDER:
            gather_copy(dq, cc).start()
        gathered[q] = spread[pl.ds(pl.multiple_of((2 * q + c) * SPREAD, SPREAD), SPREAD), :]

    landed(sib, sib_ss)
    landed(qsib, qsib_ss)
    small_copy.wait_send()
    landed(ring.at[pl.ds(0, 14)], ring_ss)
    for i in range(2):

        @pl.when(z != 2 * c + i)
        def _():
            z_copy(i).wait_send()
            landed(zq.at[0], zq_ss.at[i])

    @pl.when(active)
    def _():
        landed(yq.at[pl.ds(0, 7)], yq_ss)
        landed(p1, p1_ss)
        own = m1[8:16, :]
        same_m, same_z, other = own, own, jnp.zeros((8, 128), F32)
        same_m_top = m1[0:8, :]
        landed(p1, p1_rs)
        for dz, dm in FIRST_ORDER:
            tile = slot_of(dz, dm)
            if dm == 0:
                both = p1[tile, :]
                same_m = same_m + both[8:16, :]
                same_m_top = same_m_top + both[0:8, :]
            elif dz == 0:
                same_z = same_z + p1[tile, :]
            else:
                other = other + p1[tile, :]
        everyone = same_m + same_z - own + other
        m2[0:8, :] = same_m_top
        m2[8:16, :] = jnp.where(sub8 == 0, same_m, jnp.where(sub8 < 4, everyone, same_z))
        for dy, cc in SECOND_ORDER:
            second_copy(dy, cc).start()
        p2[y] = m2[...]
        landed(spread.at[pl.ds(0, 7 * SPREAD)], g_ss)
        landed(spread.at[pl.ds(0, 15 * 16)], p2_ss)

    landed(gathered.at[pl.ds(0, 3)], g_rs)

    @pl.when(jnp.logical_not(active))
    def _():
        landed(gathered.at[0], g_own)
        landed(p2.at[0], p2_own)

    landed(p2.at[pl.ds(0, 7)], p2_rs)
    for qq in range(4):
        out_ref[qq * SPREAD : (qq + 1) * SPREAD, :] = gathered[qq]
        out_ref[GATHERED + qq * 16 : GATHERED + qq * 16 + 16, :] = p2[qq] + p2[4 + qq]
    all_y = p2[0, 8:16, :]
    for yy in range(1, 8):
        all_y = all_y + p2[yy, 8:16, :]
    same_h = p2[4 * h, 8:16, :]
    for qq in range(1, 4):
        same_h = same_h + p2[4 * h + qq, 8:16, :]
    mine = jnp.sum(jnp.where(lane8 == 2 * q + c, same_h, 0.0), axis=1, keepdims=True)
    out_ref[SUMS : SUMS + 8, :] = jnp.where(sub8 < 4, all_y, jnp.broadcast_to(mine, (8, 128)))


def finish_kernel(
    sums_ref, matrix_ref, momentum_ref, row_factor_ref, row_rest_ref, col_factor_ref, col_rest_ref,
    new_matrix_ref, new_momentum_ref, new_row_ref, new_col_ref,
):
    entries = float(ROWS) * float(BLOCK_COLS)
    total = sums_ref[SUMS + 1 : SUMS + 2, :]
    matrix_sq = sums_ref[SUMS + 2 : SUMS + 3, :]
    base = sums_ref[SUMS + 3 : SUMS + 4, :] * 0.125
    row_mean = (base + (1.0 - beta_two) * (total / FULL_COLS)) / ROWS
    step = (1.0 - beta_one) * rel_step * jnp.sqrt(matrix_sq / entries)
    row_sums = sums_ref[SUMS + 4 : SUMS + 7, :]
    sub = lax.broadcasted_iota(jnp.int32, (3, 128), 0)

    def down(ref):
        return jnp.where(sub == 0, ref[0], jnp.where(sub == 1, ref[1], ref[2]))

    new_row = beta_two * down(row_factor_ref) + (1.0 - beta_two) * ((row_sums + down(row_rest_ref)) / FULL_COLS)
    for j in range(3):
        new_row_ref[j] = new_row[j, 0]
    row_scale = lax.rsqrt(new_row / row_mean) * step
    for qq in range(4):
        at = slice(qq * LANE_TILES, (qq + 1) * LANE_TILES)
        column_sum = sums_ref[GATHERED + qq * 16 : GATHERED + qq * 16 + LANE_TILES, :]
        new_col = beta_two * col_factor_ref[at, :] + (1.0 - beta_two) * (
            (column_sum + col_rest_ref[at, :]) / FULL_ROWS
        )
        new_col_ref[at, :] = new_col
        inverse_col = lax.rsqrt(new_col)
        for lb in range(LANE_TILES):
            b = (qq * LANE_TILES + lb) * 128
            g = sums_ref[pl.ds(qq * SPREAD + lb, 3, stride=LANE_TILES), :]
            change = g * row_scale * inverse_col[lb : lb + 1, :]
            new_momentum = beta_one * momentum_ref[:, b : b + 128] + change
            new_momentum_ref[:, b : b + 128] = new_momentum
            new_matrix_ref[:, b : b + 128] = matrix_ref[:, b : b + 128] - new_momentum


def on_device(inputs, cotangent, matrix, momentum, row_factor, col_factor, row_rest, col_rest):
    vmem = pl.BlockSpec(memory_space=VMEM)
    smem = pl.BlockSpec(memory_space=pltpu.SMEM)
    hbm = pl.BlockSpec(memory_space=pltpu.HBM)
    dma = pltpu.SemaphoreType.DMA
    sums = pl.pallas_call(
        reduce_kernel,
        out_shape=jax.ShapeDtypeStruct((SUMS + 8, 128), F32),
        in_specs=[hbm] * 5,
        out_specs=vmem,
        scratch_shapes=[
            VMEM((ROWS, 480), jnp.bfloat16),
            VMEM((3, 4608), F32),
            pltpu.SMEM((3,), F32),
            pltpu.SMEM((3,), F32),
            VMEM((ROWS, 480), jnp.bfloat16),
            VMEM((4, 480, GROUP), jnp.bfloat16),
            VMEM((2, 8, 2, A_ROWS, 128), F32),
            VMEM((8, 2, A_ROWS, 128), F32),
            VMEM((2, 4, 2, 2, B_ROWS, 128), F32),
            VMEM((4, 2, 2, B_ROWS, 128), F32),
            VMEM((16, A_ROWS, 128), F32),
            VMEM((4, A_ROWS, 128), F32),
            VMEM((4, 4, 2, B_ROWS, 128), F32),
            VMEM((8, B_ROWS, 128), F32),
            VMEM((8 * SPREAD, 128), F32),
            VMEM((4, SPREAD, 128), F32),
            VMEM((8, 128), F32),
            VMEM((8, 128), F32),
            VMEM((16, 128), F32),
            VMEM((272, 128), F32),
            VMEM((16, 128), F32),
            VMEM((8, 16, 128), F32),
            dma, dma((3,)), dma((4,)),
            dma, dma((8,)), dma, dma((4,)), dma, dma, dma, dma((2, 2, 4)),
            dma((2,)), dma, dma((2,)), dma, dma, dma, dma, dma, dma, dma, dma, dma, dma, dma,
        ],
        compiler_params=pltpu.CompilerParams(
            collective_id=0, has_side_effects=True, vmem_limit_bytes=64 * 1024 * 1024 - 65536
        ),
        name="reduce",
    )(inputs.T, cotangent, matrix, row_factor, row_rest)
    new_matrix, new_momentum, new_row, new_col = pl.pallas_call(
        finish_kernel,
        out_shape=(
            jax.ShapeDtypeStruct(matrix.shape, F32),
            jax.ShapeDtypeStruct(matrix.shape, F32),
            jax.ShapeDtypeStruct((3,), F32),
            jax.ShapeDtypeStruct((36, 128), F32),
        ),
        in_specs=[vmem, vmem, vmem, smem, smem, vmem, vmem],
        out_specs=(vmem, vmem, smem, vmem),
        name="finish",
    )(sums, matrix, momentum, row_factor, row_rest, col_factor.reshape(36, 128), col_rest.reshape(36, 128))
    return (new_matrix, new_momentum, new_row, new_col.reshape(4608))


def solution(mesh):
    placed = (
        P("dp", None),
        P("dp", "mp"),
        P("dp", "mp"),
        P("dp", "mp"),
        P("dp"),
        P("mp"),
        P("dp"),
        P("mp"),
    )
    return jax.shard_map(
        on_device,
        mesh=mesh,
        in_specs=placed,
        out_specs=(P("dp", "mp"), P("dp", "mp"), P("dp"), P("mp")),
        check_vma=False,
    )
```

```python
import functools

import jax
import jax.numpy as jnp
from jax import lax
from jax.experimental import pallas as pl
from jax.experimental.pallas import tpu as pltpu
from jax.sharding import PartitionSpec as P

FULL_ROWS = 18432
FULL_COLS = 73728
ROWS = 192
BLOCK_COLS = 36864

beta_two = 1.0 - 10.0 ** (-0.8)
beta_one = 0.9
rel_step = 0.01
eps_sq = 1e-30

MESH = pl.DeviceIdType.MESH
F32 = jnp.float32
VMEM = pltpu.VMEM

LANE_TILES = 9
A_LANES = 6
A_ROWS = A_LANES * 24
B_ROWS = (LANE_TILES - A_LANES) * 24
GROUP = LANE_TILES * 128
SPREAD = 32
STREAMS = ((0, 0, 1, 4), (1, 0, -1, 4), (0, 1, -1, 3), (1, 1, 1, 3))
GROUP_ORDER = (0, 1, 3, 2)
GATHERED = 4 * SPREAD
SUMS = GATHERED + 4 * 16
FIRST_ORDER = tuple((dz, dm) for dm in (6, 5, 7, 2, 4, 1, 3, 0) for dz in (2, 1, 3, 0) if dz or dm)
SECOND_ORDER = tuple((dy, cc) for dy in (4, 3, 5, 2, 6, 1, 7, 0) for cc in (0, 1) if dy or cc)

GATHER_ORDER = ((2, 0), (2, 1), (1, 0), (1, 1), (3, 0), (3, 1), (0, 1))
Y_AT = 5


def slot_of(dz, dm):
    if dm == 0:
        return pl.ds((dz - 1) * 16, 16)
    return pl.ds(48 + (dz * 7 + dm - 1) * 8, 8)


def send(src, dst, send_sem, recv_sem, target):
    return pltpu.make_async_remote_copy(
        src_ref=src, dst_ref=dst, send_sem=send_sem, recv_sem=recv_sem, device_id=target, device_id_type=MESH
    )


def landed(ref, sem):
    pltpu.make_async_copy(ref, ref, sem).wait()


def reduce_kernel(
    inputs_hbm, cot_hbm, matrix_hbm, row_factor_hbm, row_rest_hbm, momentum_hbm, col_factor_hbm, col_rest_hbm,
    new_matrix_ref, new_momentum_ref, new_row_ref, new_col_ref,
    inp, matrix_ref, row_factor_ref, row_rest_ref, momentum_ref, col_factor_ref, col_rest_ref, sums_ref, lhs, cot, part, sib, qpart, qsib, ring, zrecv, zq, yq,
    spread, gathered, small, small_recv, m1, p1, m2, p2,
    in_sem, late_sem, cot_sem, sib_ss, sib_rs, qsib_ss, qsib_rs, small_ss, small_rs, ring_ss, ring_rs,
    z_ss, z_rs, zq_ss, zq_rs, yq_ss, yq_rs, g_ss, g_rs, g_own, p1_ss, p1_rs, p2_ss, p2_rs, p2_own,
):
    d = lax.axis_index("dp")
    m = lax.axis_index("mp")
    z = d // 16
    y = lax.rem(d // 2, 8)
    c = lax.rem(d, 2)
    h = y // 4
    q = lax.rem(y, 4)
    home = z // 2
    active = c == home

    def dev(zz, yy, cc, mm):
        return (zz * 16 + yy * 2 + cc, mm)

    def turn(v, k, n):
        return lax.rem(v + k + n, n)

    in_copy = pltpu.make_async_copy(inputs_hbm, inp, in_sem)
    in_copy.start()
    late_copies = []
    for n, (src, dst) in enumerate(
        (
            (matrix_hbm, matrix_ref),
            (row_factor_hbm, row_factor_ref),
            (row_rest_hbm, row_rest_ref),
            (momentum_hbm, momentum_ref),
            (col_factor_hbm, col_factor_ref),
            (col_rest_hbm, col_rest_ref),
        )
    ):
        late_copies.append(pltpu.make_async_copy(src, dst, late_sem.at[n]))
    cot_copies = []
    for n, off in enumerate(GROUP_ORDER):
        g = turn(q, off, 4)
        copy = pltpu.make_async_copy(
            cot_hbm.at[:, pl.ds(pl.multiple_of(g * GROUP, 128), GROUP)], cot.at[n], cot_sem.at[n]
        )
        cot_copies.append(copy)
    cot_copies[0].start()

    barrier = pltpu.get_barrier_semaphore()

    def hello(target):
        pl.semaphore_signal(barrier, inc=1, device_id=target, device_id_type=MESH)

    @pl.when(active)
    def _():
        for dz, dm in FIRST_ORDER:
            zz = turn(z, dz, 4)
            hello(dev(zz, y, zz // 2, turn(m, dm, 8)))
        for i in range(2):
            hello(dev((1 - home) * 2 + i, y, c, m))

    @pl.when(jnp.logical_not(active))
    def _():
        for i in range(2):
            hello(dev(2 * c + i, y, c, m))

    for dy, cc in SECOND_ORDER:
        hello(dev(z, turn(y, dy, 8), lax.rem(c + cc, 2), m))

    row = lax.broadcasted_iota(jnp.int32, (ROWS, ROWS), 0)
    col = lax.broadcasted_iota(jnp.int32, (ROWS, ROWS), 1)
    block = (row * 2731) >> 16
    inner = row - block * 24
    want = block * 24 + 3 * (inner & 7) + (inner >> 3)
    pick = jnp.where(col == want, 1.0, 0.0).astype(jnp.bfloat16)
    in_copy.wait()
    cot_copies[1].start()
    lhs[...] = jnp.dot(pick, inp[...], preferred_element_type=F32).astype(jnp.bfloat16)

    sub8 = lax.broadcasted_iota(jnp.int32, (8, 128), 0)
    lane8 = lax.broadcasted_iota(jnp.int32, (8, 128), 1)

    def product(n):
        cot_copies[n].wait()
        if n < 2:
            cot_copies[n + 2].start()
        if n == 2:
            for copy in late_copies:
                copy.start()
        g = turn(q, GROUP_ORDER[n], 4)
        acc = jnp.dot(lhs[...], cot[n], preferred_element_type=F32)
        for zh in range(2):
            for i in range(2):
                for hh in range(2):
                    r0 = ((zh * 2 + i) * 2 + hh) * 24
                    for lb in range(LANE_TILES):
                        for j in range(3):
                            tile = acc[r0 + j * 8 : r0 + j * 8 + 8, lb * 128 : lb * 128 + 128]
                            if lb < A_LANES:
                                t = (lb * 3 + j) * 8
                                part[zh, hh * 4 + g, i, t : t + 8, :] = tile
                            else:
                                t = ((lb - A_LANES) * 3 + j) * 8
                                qpart[zh, g, i, hh, t : t + 8, :] = tile

    sibling = dev(z, y, 1 - c, m)

    def sib_copy(o):
        return send(part.at[1 - c, o], sib.at[o], sib_ss, sib_rs.at[o], sibling)

    def qsib_copy(g):
        return send(qpart.at[1 - c, g], qsib.at[g], qsib_ss, qsib_rs.at[g], sibling)

    small_copy = send(small, small_recv, small_ss, small_rs, sibling)

    def pass_on(n):
        for off in (4, 0):
            sib_copy(turn(y, GROUP_ORDER[n] + off, 8)).start()
        qsib_copy(turn(q, GROUP_ORDER[n], 4)).start()

    def zq_copy(g, i):
        return send(qpart.at[c, g, i], zq.at[z, g], zq_ss.at[i], zq_rs, dev(2 * c + i, y, c, m))

    def along_z(n):
        g = turn(q, GROUP_ORDER[n], 4)
        qsib_copy(g).wait_recv()
        for i in range(2):
            qpart[c, g, i] = qpart[c, g, i] + qsib[g, i]

            @pl.when(z != 2 * c + i)
            def _():
                zq_copy(g, i).start()

    arrived = set()

    def arrive(k):
        k %= 8
        if k not in arrived:
            arrived.add(k)
            sib_copy(turn(y, k, 8)).wait_recv()

    def ring_copy(stream, s):
        i, kind, way, n = stream
        o = turn(y, (way * (n + 1 - s)) % 8, 8)
        return send(
            part.at[c, o, i],
            ring.at[(i * 2 + kind) * 4 + s - 1],
            ring_ss,
            ring_rs.at[i, kind, s - 1],
            dev(z, turn(y, way % 8, 8), c, m),
        )

    def ring_step(stream, s):
        i, kind, way, n = stream
        off = (way * (n + 1 - s)) % 8
        o = turn(y, off, 8)
        arrive(off)
        total = part[c, o, i] + sib[o, i]
        if s > 1:
            ring_copy(stream, s - 1).wait_recv()
            total = total + ring[(i * 2 + kind) * 4 + s - 2]
        part[c, o, i] = total
        ring_copy(stream, s).start()

    product(0)
    pl.semaphore_wait(barrier, jnp.where(active, 48, 17))
    pass_on(0)
    product(1)
    pass_on(1)
    ring_step(STREAMS[0], 1)
    ring_step(STREAMS[1], 1)
    product(2)
    pass_on(2)
    ring_step(STREAMS[2], 1)
    along_z(0)
    product(3)
    pass_on(3)
    ring_step(STREAMS[3], 1)
    for n in (1, 2, 3):
        along_z(n)

    for copy in late_copies:
        copy.wait()
    mat = matrix_ref[...]
    msq = jnp.sum(jnp.sum(mat * mat, axis=0, keepdims=True), axis=1, keepdims=True)
    base = jnp.float32(0.0)
    for j in range(3):
        base = base + beta_two * row_factor_ref[j] + (1.0 - beta_two) * (row_rest_ref[j] * (1.0 / FULL_COLS))
    small[...] = jnp.where(sub8 == 2, msq, jnp.where(sub8 == 3, base, 0.0))

    small_copy.start()

    def yq_copy(g, hh):
        return send(
            qpart.at[c, g, z - 2 * home, hh], yq.at[y], yq_ss, yq_rs, dev(z, 4 * hh + g, c, m)
        )

    def along_y():
        @pl.when(active)
        def _():
            landed(zq.at[pl.ds(0, 3)], zq_rs)
            for dy in (4, 3, 5, 2, 6, 1, 7, 0):
                yy = turn(y, dy, 8)
                g, hh = lax.rem(yy, 4), yy // 4
                total = qpart[c, g, z - 2 * home, hh]
                for dz in range(1, 4):
                    total = total + zq[turn(z, dz, 4), g, hh]
                if dy:
                    qpart[c, g, z - 2 * home, hh] = total
                    yq_copy(g, hh).start()
                else:
                    yq[y] = total

    for s in range(2, 5):
        if s == Y_AT:
            along_y()
        for stream in STREAMS:
            if s <= stream[3]:
                ring_step(stream, s)
    if Y_AT > 4:
        along_y()

    arrive(0)

    def z_copy(i):
        return send(part.at[c, y, i], zrecv.at[z], z_ss.at[i], z_rs, dev(2 * c + i, y, c, m))

    for i in range(2):
        ring_copy(STREAMS[2 + i], 3).wait_recv()
        ring_copy(STREAMS[i], 4).wait_recv()
        total = part[c, y, i] + sib[y, i] + ring[i * 8 + 3] + ring[i * 8 + 6]

        @pl.when(z != 2 * c + i)
        def _():
            part[c, y, i] = total
            z_copy(i).start()

        @pl.when(z == 2 * c + i)
        def _():
            zrecv[z] = total

    small_copy.wait_recv()

    def first_copy(dz, dm):
        zz = turn(z, dz, 4)
        rows = pl.ds(0, 16) if dm == 0 else pl.ds(8, 8)
        slot = slot_of((4 - dz) % 4, (8 - dm) % 8)
        return send(m1.at[rows], p1.at[slot], p1_ss, p1_rs, dev(zz, y, zz // 2, turn(m, dm, 8)))

    def gather_copy(dq, cc):
        k = 2 * turn(q, dq, 4) + lax.rem(c + cc, 2)
        return send(
            spread.at[pl.ds(pl.multiple_of(k * SPREAD, SPREAD), SPREAD)],
            gathered.at[q],
            g_ss,
            g_rs if dq else g_own,
            dev(z, 4 * h + turn(q, dq, 4), lax.rem(c + cc, 2), m),
        )

    def second_copy(dy, cc):
        return send(
            m2, p2.at[y], p2_ss, p2_rs if dy else p2_own, dev(z, turn(y, dy, 8), lax.rem(c + cc, 2), m)
        )

    @pl.when(active)
    def _():
        landed(yq.at[pl.ds(0, 7)], yq_rs)
        landed(zrecv.at[pl.ds(0, 3)], z_rs)
        column = [None] * LANE_TILES
        rows = [None] * 3
        for lb in range(LANE_TILES):
            for j in range(3):
                if lb < A_LANES:
                    t = (lb * 3 + j) * 8
                    at = slice(t, t + 8)
                    g = (zrecv[0, at] + zrecv[1, at]) + (zrecv[2, at] + zrecv[3, at])
                else:
                    t = ((lb - A_LANES) * 3 + j) * 8
                    at = slice(t, t + 8)
                    g = ((yq[0, at] + yq[1, at]) + (yq[2, at] + yq[3, at])) + (
                        (yq[4, at] + yq[5, at]) + (yq[6, at] + yq[7, at])
                    )
                spread[pl.ds(j * LANE_TILES + lb, 8, stride=SPREAD), :] = g
                square = g * g + eps_sq
                column[lb] = square if j == 0 else column[lb] + square
                rows[j] = square if lb == 0 else rows[j] + square
        for lb in range(LANE_TILES):
            m1[lb : lb + 1, :] = jnp.sum(column[lb], axis=0, keepdims=True)
        every = jnp.sum(rows[0] + rows[1] + rows[2], axis=0, keepdims=True)
        m1[9:10, :] = jnp.broadcast_to(jnp.sum(every, axis=1, keepdims=True), (1, 128))
        m1[10:12, :] = small[2:4, :] + small_recv[2:4, :]
        for j in range(3):
            each = jnp.broadcast_to(jnp.sum(rows[j], axis=1, keepdims=True), (8, 128))
            m1[12 + j : 13 + j, :] = jnp.sum(jnp.where(lane8 == sub8, each, 0.0), axis=0, keepdims=True)
        m1[15:16, :] = jnp.zeros((1, 128), F32)
        for dz, dm in FIRST_ORDER:
            first_copy(dz, dm).start()
        for dq, cc in GATHER_ORDER:
            gather_copy(dq, cc).start()
        gathered[q] = spread[pl.ds(pl.multiple_of((2 * q + c) * SPREAD, SPREAD), SPREAD), :]

    landed(sib, sib_ss)
    landed(qsib, qsib_ss)
    small_copy.wait_send()
    landed(ring.at[pl.ds(0, 14)], ring_ss)
    for i in range(2):

        @pl.when(z != 2 * c + i)
        def _():
            z_copy(i).wait_send()
            landed(zq.at[0], zq_ss.at[i])

    @pl.when(active)
    def _():
        landed(yq.at[pl.ds(0, 7)], yq_ss)
        landed(p1, p1_ss)
        own = m1[8:16, :]
        same_m, same_z, other = own, own, jnp.zeros((8, 128), F32)
        same_m_top = m1[0:8, :]
        landed(p1, p1_rs)
        for dz, dm in FIRST_ORDER:
            tile = slot_of(dz, dm)
            if dm == 0:
                both = p1[tile, :]
                same_m = same_m + both[8:16, :]
                same_m_top = same_m_top + both[0:8, :]
            elif dz == 0:
                same_z = same_z + p1[tile, :]
            else:
                other = other + p1[tile, :]
        everyone = same_m + same_z - own + other
        m2[0:8, :] = same_m_top
        m2[8:16, :] = jnp.where(sub8 == 0, same_m, jnp.where(sub8 < 4, everyone, same_z))
        for dy, cc in SECOND_ORDER:
            second_copy(dy, cc).start()
        p2[y] = m2[...]
        landed(spread.at[pl.ds(0, 7 * SPREAD)], g_ss)
        landed(spread.at[pl.ds(0, 15 * 16)], p2_ss)

    landed(gathered.at[pl.ds(0, 3)], g_rs)

    @pl.when(jnp.logical_not(active))
    def _():
        landed(gathered.at[0], g_own)
        landed(p2.at[0], p2_own)

    landed(p2.at[pl.ds(0, 7)], p2_rs)
    for qq in range(4):
        sums_ref[qq * SPREAD : (qq + 1) * SPREAD, :] = gathered[qq]
        sums_ref[GATHERED + qq * 16 : GATHERED + qq * 16 + 16, :] = p2[qq] + p2[4 + qq]
    all_y = p2[0, 8:16, :]
    for yy in range(1, 8):
        all_y = all_y + p2[yy, 8:16, :]
    same_h = p2[4 * h, 8:16, :]
    for qq in range(1, 4):
        same_h = same_h + p2[4 * h + qq, 8:16, :]
    mine = jnp.sum(jnp.where(lane8 == 2 * q + c, same_h, 0.0), axis=1, keepdims=True)
    sums_ref[SUMS : SUMS + 8, :] = jnp.where(sub8 < 4, all_y, jnp.broadcast_to(mine, (8, 128)))

    entries = float(ROWS) * float(BLOCK_COLS)
    total = sums_ref[SUMS + 1 : SUMS + 2, :]
    matrix_sq = sums_ref[SUMS + 2 : SUMS + 3, :]
    base = sums_ref[SUMS + 3 : SUMS + 4, :] * 0.125
    row_mean = (base + (1.0 - beta_two) * (total / FULL_COLS)) / ROWS
    step = (1.0 - beta_one) * rel_step * jnp.sqrt(matrix_sq / entries)
    row_sums = sums_ref[SUMS + 4 : SUMS + 7, :]
    sub = lax.broadcasted_iota(jnp.int32, (3, 128), 0)

    def down(ref):
        return jnp.where(sub == 0, ref[0], jnp.where(sub == 1, ref[1], ref[2]))

    new_row = beta_two * down(row_factor_ref) + (1.0 - beta_two) * ((row_sums + down(row_rest_ref)) / FULL_COLS)
    new_row_ref[0:3, :] = new_row
    row_scale = lax.rsqrt(new_row / row_mean) * step
    for qq in range(4):
        at = slice(qq * LANE_TILES, (qq + 1) * LANE_TILES)
        column_sum = sums_ref[GATHERED + qq * 16 : GATHERED + qq * 16 + LANE_TILES, :]
        new_col = beta_two * col_factor_ref[at, :] + (1.0 - beta_two) * (
            (column_sum + col_rest_ref[at, :]) / FULL_ROWS
        )
        new_col_ref[at, :] = new_col
        inverse_col = lax.rsqrt(new_col)
        for lb in range(LANE_TILES):
            b = (qq * LANE_TILES + lb) * 128
            g = sums_ref[pl.ds(qq * SPREAD + lb, 3, stride=LANE_TILES), :]
            change = g * row_scale * inverse_col[lb : lb + 1, :]
            new_momentum = beta_one * momentum_ref[:, b : b + 128] + change
            new_momentum_ref[:, b : b + 128] = new_momentum
            new_matrix_ref[:, b : b + 128] = matrix_ref[:, b : b + 128] - new_momentum


def place_kernel(
    matrix_ref, momentum_ref, row_ref, col_ref, new_matrix_ref, new_momentum_ref, new_row_ref, new_col_ref, sem
):
    copies = []
    for n, (src, dst) in enumerate(
        ((matrix_ref, new_matrix_ref), (momentum_ref, new_momentum_ref), (col_ref, new_col_ref))
    ):
        copy = pltpu.make_async_copy(src, dst, sem.at[n])
        copy.start()
        copies.append(copy)
    for j in range(3):
        new_row_ref[j] = row_ref[j : j + 1, 0:1][0, 0]
    for copy in copies:
        copy.wait()


def on_device(inputs, cotangent, matrix, momentum, row_factor, col_factor, row_rest, col_rest):
    vmem = pl.BlockSpec(memory_space=VMEM)
    smem = pl.BlockSpec(memory_space=pltpu.SMEM)
    hbm = pl.BlockSpec(memory_space=pltpu.HBM)
    dma = pltpu.SemaphoreType.DMA
    held = pltpu.with_memory_space_constraint
    done = pl.pallas_call(
        reduce_kernel,
        out_shape=(
            jax.ShapeDtypeStruct(matrix.shape, F32),
            jax.ShapeDtypeStruct(matrix.shape, F32),
            jax.ShapeDtypeStruct((8, 128), F32),
            jax.ShapeDtypeStruct((36, 128), F32),
        ),
        in_specs=[hbm] * 8,
        out_specs=(vmem,) * 4,
        scratch_shapes=[
            VMEM((ROWS, 480), jnp.bfloat16),
            VMEM((3, 4608), F32),
            pltpu.SMEM((3,), F32),
            pltpu.SMEM((3,), F32),
            VMEM((3, 4608), F32),
            VMEM((36, 128), F32),
            VMEM((36, 128), F32),
            VMEM((SUMS + 8, 128), F32),
            VMEM((ROWS, 480), jnp.bfloat16),
            VMEM((4, 480, GROUP), jnp.bfloat16),
            VMEM((2, 8, 2, A_ROWS, 128), F32),
            VMEM((8, 2, A_ROWS, 128), F32),
            VMEM((2, 4, 2, 2, B_ROWS, 128), F32),
            VMEM((4, 2, 2, B_ROWS, 128), F32),
            VMEM((16, A_ROWS, 128), F32),
            VMEM((4, A_ROWS, 128), F32),
            VMEM((4, 4, 2, B_ROWS, 128), F32),
            VMEM((8, B_ROWS, 128), F32),
            VMEM((8 * SPREAD, 128), F32),
            VMEM((4, SPREAD, 128), F32),
            VMEM((8, 128), F32),
            VMEM((8, 128), F32),
            VMEM((16, 128), F32),
            VMEM((272, 128), F32),
            VMEM((16, 128), F32),
            VMEM((8, 16, 128), F32),
            dma, dma((6,)), dma((4,)),
            dma, dma((8,)), dma, dma((4,)), dma, dma, dma, dma((2, 2, 4)),
            dma((2,)), dma, dma((2,)), dma, dma, dma, dma, dma, dma, dma, dma, dma, dma, dma,
        ],
        compiler_params=pltpu.CompilerParams(
            collective_id=0, has_side_effects=True, vmem_limit_bytes=40 * 1024 * 1024
        ),
        name="reduce",
    )(
        *[
            held(v, pltpu.HBM)
            for v in (
                inputs.T, cotangent, matrix, row_factor, row_rest, momentum,
                col_factor.reshape(36, 128), col_rest.reshape(36, 128),
            )
        ]
    )
    new_matrix, new_momentum, new_row, new_col = pl.pallas_call(
        place_kernel,
        out_shape=(
            jax.ShapeDtypeStruct(matrix.shape, F32),
            jax.ShapeDtypeStruct(matrix.shape, F32),
            jax.ShapeDtypeStruct((3,), F32),
            jax.ShapeDtypeStruct((36, 128), F32),
        ),
        in_specs=[vmem] * 4,
        out_specs=(hbm, hbm, smem, hbm),
        scratch_shapes=[dma((3,))],
        name="place",
    )(*[held(v, VMEM) for v in done])
    return (new_matrix, new_momentum, new_row, new_col.reshape(4608))


def solution(mesh):
    placed = (
        P("dp", None),
        P("dp", "mp"),
        P("dp", "mp"),
        P("dp", "mp"),
        P("dp"),
        P("mp"),
        P("dp"),
        P("mp"),
    )
    return jax.shard_map(
        on_device,
        mesh=mesh,
        in_specs=placed,
        out_specs=(P("dp", "mp"), P("dp", "mp"), P("dp"), P("mp")),
        check_vma=False,
    )
```

```python
import functools

import jax
import jax.numpy as jnp
from jax import lax
from jax.experimental import pallas as pl
from jax.experimental.pallas import tpu as pltpu
from jax.sharding import PartitionSpec as P

FULL_ROWS = 18432
FULL_COLS = 73728
ROWS = 192
BLOCK_COLS = 36864

beta_two = 1.0 - 10.0 ** (-0.8)
beta_one = 0.9
rel_step = 0.01
eps_sq = 1e-30

MESH = pl.DeviceIdType.MESH
F32 = jnp.float32
VMEM = pltpu.VMEM

LANE_TILES = 9
A_LANES = 6
A_ROWS = A_LANES * 24
B_ROWS = (LANE_TILES - A_LANES) * 24
GROUP = LANE_TILES * 128
SPREAD = 32
STREAMS = ((0, 0, 1, 4), (1, 0, -1, 4), (0, 1, -1, 3), (1, 1, 1, 3))
GROUP_ORDER = (0, 1, 3, 2)
GATHERED = 4 * SPREAD
SUMS = GATHERED + 4 * 16
FIRST_ORDER = tuple((dz, dm) for dm in (6, 5, 7, 2, 4, 1, 3, 0) for dz in (2, 1, 3, 0) if dz or dm)
SECOND_ORDER = tuple((dy, cc) for dy in (4, 3, 5, 2, 6, 1, 7, 0) for cc in (0, 1) if dy or cc)

GATHER_ORDER = ((2, 0), (2, 1), (1, 0), (1, 1), (3, 0), (3, 1), (0, 1))
Y_AT = 5


def slot_of(dz, dm):
    if dm == 0:
        return pl.ds((dz - 1) * 16, 16)
    return pl.ds(48 + (dz * 7 + dm - 1) * 8, 8)


def send(src, dst, send_sem, recv_sem, target):
    return pltpu.make_async_remote_copy(
        src_ref=src, dst_ref=dst, send_sem=send_sem, recv_sem=recv_sem, device_id=target, device_id_type=MESH
    )


def landed(ref, sem):
    pltpu.make_async_copy(ref, ref, sem).wait()


def reduce_kernel(
    inputs_hbm, cot_hbm, matrix_hbm, row_factor_hbm, row_rest_hbm, momentum_hbm, col_factor_hbm, col_rest_hbm,
    new_matrix_ref, new_momentum_ref, new_row_ref, new_col_ref,
    inp, matrix_ref, row_factor_ref, row_rest_ref, momentum_ref, col_factor_ref, col_rest_ref, sums_ref, lhs, cot, part, sib, qpart, qsib, ring, zrecv, zq, yq,
    spread, gathered, small, small_recv, m1, p1, m2, p2,
    in_sem, late_sem, cot_sem, sib_ss, sib_rs, qsib_ss, qsib_rs, small_ss, small_rs, ring_ss, ring_rs,
    z_ss, z_rs, zq_ss, zq_rs, yq_ss, yq_rs, g_ss, g_rs, g_own, p1_ss, p1_rs, p2_ss, p2_rs, p2_own,
):
    d = lax.axis_index("dp")
    m = lax.axis_index("mp")
    z = d // 16
    y = lax.rem(d // 2, 8)
    c = lax.rem(d, 2)
    h = y // 4
    q = lax.rem(y, 4)
    home = z // 2
    active = c == home

    def dev(zz, yy, cc, mm):
        return (zz * 16 + yy * 2 + cc, mm)

    def turn(v, k, n):
        return lax.rem(v + k + n, n)

    in_copy = pltpu.make_async_copy(inputs_hbm, inp, in_sem)
    in_copy.start()
    late_copies = []
    for n, (src, dst) in enumerate(
        (
            (matrix_hbm, matrix_ref),
            (row_factor_hbm, row_factor_ref),
            (row_rest_hbm, row_rest_ref),
            (momentum_hbm, momentum_ref),
            (col_factor_hbm, col_factor_ref),
            (col_rest_hbm, col_rest_ref),
        )
    ):
        late_copies.append(pltpu.make_async_copy(src, dst, late_sem.at[n]))
    cot_copies = []
    for n, off in enumerate(GROUP_ORDER):
        g = turn(q, off, 4)
        copy = pltpu.make_async_copy(
            cot_hbm.at[:, pl.ds(pl.multiple_of(g * GROUP, 128), GROUP)], cot.at[n], cot_sem.at[n]
        )
        cot_copies.append(copy)
    cot_copies[0].start()

    barrier = pltpu.get_barrier_semaphore()

    def hello(target):
        pl.semaphore_signal(barrier, inc=1, device_id=target, device_id_type=MESH)

    @pl.when(active)
    def _():
        for dz, dm in FIRST_ORDER:
            zz = turn(z, dz, 4)
            hello(dev(zz, y, zz // 2, turn(m, dm, 8)))
        for i in range(2):
            hello(dev((1 - home) * 2 + i, y, c, m))

    @pl.when(jnp.logical_not(active))
    def _():
        for i in range(2):
            hello(dev(2 * c + i, y, c, m))

    for dy, cc in SECOND_ORDER:
        hello(dev(z, turn(y, dy, 8), lax.rem(c + cc, 2), m))

    row = lax.broadcasted_iota(jnp.int32, (ROWS, ROWS), 0)
    col = lax.broadcasted_iota(jnp.int32, (ROWS, ROWS), 1)
    block = (row * 2731) >> 16
    inner = row - block * 24
    want = block * 24 + 3 * (inner & 7) + (inner >> 3)
    pick = jnp.where(col == want, 1.0, 0.0).astype(jnp.bfloat16)
    in_copy.wait()
    cot_copies[1].start()
    lhs[...] = jnp.dot(pick, inp[...], preferred_element_type=F32).astype(jnp.bfloat16)

    sub8 = lax.broadcasted_iota(jnp.int32, (8, 128), 0)
    lane8 = lax.broadcasted_iota(jnp.int32, (8, 128), 1)

    def product(n):
        cot_copies[n].wait()
        if n < 2:
            cot_copies[n + 2].start()
        if n == 2:
            for copy in late_copies:
                copy.start()
        g = turn(q, GROUP_ORDER[n], 4)
        acc = jnp.dot(lhs[...], cot[n], preferred_element_type=F32)
        for zh in range(2):
            for i in range(2):
                for hh in range(2):
                    r0 = ((zh * 2 + i) * 2 + hh) * 24
                    for lb in range(LANE_TILES):
                        for j in range(3):
                            tile = acc[r0 + j * 8 : r0 + j * 8 + 8, lb * 128 : lb * 128 + 128]
                            if lb < A_LANES:
                                t = (lb * 3 + j) * 8
                                part[zh, hh * 4 + g, i, t : t + 8, :] = tile
                            else:
                                t = ((lb - A_LANES) * 3 + j) * 8
                                qpart[zh, g, i, hh, t : t + 8, :] = tile

    sibling = dev(z, y, 1 - c, m)

    def sib_copy(o):
        return send(part.at[1 - c, o], sib.at[o], sib_ss, sib_rs.at[o], sibling)

    def qsib_copy(g):
        return send(qpart.at[1 - c, g], qsib.at[g], qsib_ss, qsib_rs.at[g], sibling)

    small_copy = send(small, small_recv, small_ss, small_rs, sibling)

    def pass_on(n):
        for off in (4, 0):
            sib_copy(turn(y, GROUP_ORDER[n] + off, 8)).start()
        qsib_copy(turn(q, GROUP_ORDER[n], 4)).start()

    def zq_copy(g, i):
        return send(qpart.at[c, g, i], zq.at[z, g], zq_ss.at[i], zq_rs, dev(2 * c + i, y, c, m))

    def along_z(n):
        g = turn(q, GROUP_ORDER[n], 4)
        qsib_copy(g).wait_recv()
        for i in range(2):
            qpart[c, g, i] = qpart[c, g, i] + qsib[g, i]

            @pl.when(z != 2 * c + i)
            def _():
                zq_copy(g, i).start()

    arrived = set()

    def arrive(k):
        k %= 8
        if k not in arrived:
            arrived.add(k)
            sib_copy(turn(y, k, 8)).wait_recv()

    def ring_copy(stream, s):
        i, kind, way, n = stream
        o = turn(y, (way * (n + 1 - s)) % 8, 8)
        return send(
            part.at[c, o, i],
            ring.at[(i * 2 + kind) * 4 + s - 1],
            ring_ss,
            ring_rs.at[i, kind, s - 1],
            dev(z, turn(y, way % 8, 8), c, m),
        )

    def ring_step(stream, s):
        i, kind, way, n = stream
        off = (way * (n + 1 - s)) % 8
        o = turn(y, off, 8)
        arrive(off)
        total = part[c, o, i] + sib[o, i]
        if s > 1:
            ring_copy(stream, s - 1).wait_recv()
            total = total + ring[(i * 2 + kind) * 4 + s - 2]
        part[c, o, i] = total
        ring_copy(stream, s).start()

    product(0)
    pl.semaphore_wait(barrier, jnp.where(active, 48, 17))
    pass_on(0)
    product(1)
    pass_on(1)
    ring_step(STREAMS[0], 1)
    ring_step(STREAMS[1], 1)
    product(2)
    pass_on(2)
    ring_step(STREAMS[2], 1)
    along_z(0)
    product(3)
    pass_on(3)
    ring_step(STREAMS[3], 1)
    for n in (1, 2, 3):
        along_z(n)

    for copy in late_copies:
        copy.wait()
    mat = matrix_ref[...]
    msq = jnp.sum(jnp.sum(mat * mat, axis=0, keepdims=True), axis=1, keepdims=True)
    base = jnp.float32(0.0)
    for j in range(3):
        base = base + beta_two * row_factor_ref[j] + (1.0 - beta_two) * (row_rest_ref[j] * (1.0 / FULL_COLS))
    small[...] = jnp.where(sub8 == 2, msq, jnp.where(sub8 == 3, base, 0.0))

    small_copy.start()

    def yq_copy(g, hh):
        return send(
            qpart.at[c, g, z - 2 * home, hh], yq.at[y], yq_ss, yq_rs, dev(z, 4 * hh + g, c, m)
        )

    def along_y():
        @pl.when(active)
        def _():
            landed(zq.at[pl.ds(0, 3)], zq_rs)
            for dy in (4, 3, 5, 2, 6, 1, 7, 0):
                yy = turn(y, dy, 8)
                g, hh = lax.rem(yy, 4), yy // 4
                total = qpart[c, g, z - 2 * home, hh]
                for dz in range(1, 4):
                    total = total + zq[turn(z, dz, 4), g, hh]
                if dy:
                    qpart[c, g, z - 2 * home, hh] = total
                    yq_copy(g, hh).start()
                else:
                    yq[y] = total

    for s in range(2, 5):
        if s == Y_AT:
            along_y()
        for stream in STREAMS:
            if s <= stream[3]:
                ring_step(stream, s)
    if Y_AT > 4:
        along_y()

    arrive(0)

    def z_copy(i):
        return send(part.at[c, y, i], zrecv.at[z], z_ss.at[i], z_rs, dev(2 * c + i, y, c, m))

    for i in range(2):
        ring_copy(STREAMS[2 + i], 3).wait_recv()
        ring_copy(STREAMS[i], 4).wait_recv()
        total = part[c, y, i] + sib[y, i] + ring[i * 8 + 3] + ring[i * 8 + 6]

        @pl.when(z != 2 * c + i)
        def _():
            part[c, y, i] = total
            z_copy(i).start()

        @pl.when(z == 2 * c + i)
        def _():
            zrecv[z] = total

    small_copy.wait_recv()

    def first_copy(dz, dm):
        zz = turn(z, dz, 4)
        rows = pl.ds(0, 16) if dm == 0 else pl.ds(8, 8)
        slot = slot_of((4 - dz) % 4, (8 - dm) % 8)
        return send(m1.at[rows], p1.at[slot], p1_ss, p1_rs, dev(zz, y, zz // 2, turn(m, dm, 8)))

    def gather_copy(dq, cc):
        k = 2 * turn(q, dq, 4) + lax.rem(c + cc, 2)
        return send(
            spread.at[pl.ds(pl.multiple_of(k * SPREAD, SPREAD), SPREAD)],
            gathered.at[q],
            g_ss,
            g_rs if dq else g_own,
            dev(z, 4 * h + turn(q, dq, 4), lax.rem(c + cc, 2), m),
        )

    def second_copy(dy, cc):
        return send(
            m2, p2.at[y], p2_ss, p2_rs if dy else p2_own, dev(z, turn(y, dy, 8), lax.rem(c + cc, 2), m)
        )

    @pl.when(active)
    def _():
        landed(yq.at[pl.ds(0, 7)], yq_rs)
        landed(zrecv.at[pl.ds(0, 3)], z_rs)
        column = [None] * LANE_TILES
        rows = [None] * 3
        for lb in range(LANE_TILES):
            for j in range(3):
                if lb < A_LANES:
                    t = (lb * 3 + j) * 8
                    at = slice(t, t + 8)
                    g = (zrecv[0, at] + zrecv[1, at]) + (zrecv[2, at] + zrecv[3, at])
                else:
                    t = ((lb - A_LANES) * 3 + j) * 8
                    at = slice(t, t + 8)
                    g = ((yq[0, at] + yq[1, at]) + (yq[2, at] + yq[3, at])) + (
                        (yq[4, at] + yq[5, at]) + (yq[6, at] + yq[7, at])
                    )
                spread[pl.ds(j * LANE_TILES + lb, 8, stride=SPREAD), :] = g
                square = g * g + eps_sq
                column[lb] = square if j == 0 else column[lb] + square
                rows[j] = square if lb == 0 else rows[j] + square
        for lb in range(LANE_TILES):
            m1[lb : lb + 1, :] = jnp.sum(column[lb], axis=0, keepdims=True)
        every = jnp.sum(rows[0] + rows[1] + rows[2], axis=0, keepdims=True)
        m1[9:10, :] = jnp.broadcast_to(jnp.sum(every, axis=1, keepdims=True), (1, 128))
        m1[10:12, :] = small[2:4, :] + small_recv[2:4, :]
        for j in range(3):
            each = jnp.broadcast_to(jnp.sum(rows[j], axis=1, keepdims=True), (8, 128))
            m1[12 + j : 13 + j, :] = jnp.sum(jnp.where(lane8 == sub8, each, 0.0), axis=0, keepdims=True)
        m1[15:16, :] = jnp.zeros((1, 128), F32)
        for dz, dm in FIRST_ORDER:
            first_copy(dz, dm).start()
        for dq, cc in GATHER_ORDER:
            gather_copy(dq, cc).start()
        gathered[q] = spread[pl.ds(pl.multiple_of((2 * q + c) * SPREAD, SPREAD), SPREAD), :]

    landed(sib, sib_ss)
    landed(qsib, qsib_ss)
    small_copy.wait_send()
    landed(ring.at[pl.ds(0, 14)], ring_ss)
    for i in range(2):

        @pl.when(z != 2 * c + i)
        def _():
            z_copy(i).wait_send()
            landed(zq.at[0], zq_ss.at[i])

    @pl.when(active)
    def _():
        landed(yq.at[pl.ds(0, 7)], yq_ss)
        landed(p1, p1_ss)
        own = m1[8:16, :]
        same_m, same_z, other = own, own, jnp.zeros((8, 128), F32)
        same_m_top = m1[0:8, :]
        landed(p1, p1_rs)
        for dz, dm in FIRST_ORDER:
            tile = slot_of(dz, dm)
            if dm == 0:
                both = p1[tile, :]
                same_m = same_m + both[8:16, :]
                same_m_top = same_m_top + both[0:8, :]
            elif dz == 0:
                same_z = same_z + p1[tile, :]
            else:
                other = other + p1[tile, :]
        everyone = same_m + same_z - own + other
        m2[0:8, :] = same_m_top
        m2[8:16, :] = jnp.where(sub8 == 0, same_m, jnp.where(sub8 < 4, everyone, same_z))
        for dy, cc in SECOND_ORDER:
            second_copy(dy, cc).start()
        p2[y] = m2[...]
        landed(spread.at[pl.ds(0, 7 * SPREAD)], g_ss)
        landed(spread.at[pl.ds(0, 15 * 16)], p2_ss)

    landed(gathered.at[pl.ds(0, 3)], g_rs)

    @pl.when(jnp.logical_not(active))
    def _():
        landed(gathered.at[0], g_own)
        landed(p2.at[0], p2_own)

    landed(p2.at[pl.ds(0, 7)], p2_rs)
    for qq in range(4):
        sums_ref[qq * SPREAD : (qq + 1) * SPREAD, :] = gathered[qq]
        sums_ref[GATHERED + qq * 16 : GATHERED + qq * 16 + 16, :] = p2[qq] + p2[4 + qq]
    all_y = p2[0, 8:16, :]
    for yy in range(1, 8):
        all_y = all_y + p2[yy, 8:16, :]
    same_h = p2[4 * h, 8:16, :]
    for qq in range(1, 4):
        same_h = same_h + p2[4 * h + qq, 8:16, :]
    mine = jnp.sum(jnp.where(lane8 == 2 * q + c, same_h, 0.0), axis=1, keepdims=True)
    sums_ref[SUMS : SUMS + 8, :] = jnp.where(sub8 < 4, all_y, jnp.broadcast_to(mine, (8, 128)))

    entries = float(ROWS) * float(BLOCK_COLS)
    total = sums_ref[SUMS + 1 : SUMS + 2, :]
    matrix_sq = sums_ref[SUMS + 2 : SUMS + 3, :]
    base = sums_ref[SUMS + 3 : SUMS + 4, :] * 0.125
    row_mean = (base + (1.0 - beta_two) * (total / FULL_COLS)) / ROWS
    step = (1.0 - beta_one) * rel_step * jnp.sqrt(matrix_sq / entries)
    row_sums = sums_ref[SUMS + 4 : SUMS + 7, :]
    sub = lax.broadcasted_iota(jnp.int32, (3, 128), 0)

    def down(ref):
        return jnp.where(sub == 0, ref[0], jnp.where(sub == 1, ref[1], ref[2]))

    new_row = beta_two * down(row_factor_ref) + (1.0 - beta_two) * ((row_sums + down(row_rest_ref)) / FULL_COLS)
    new_row_ref[0:3, :] = new_row
    row_scale = lax.rsqrt(new_row / row_mean) * step
    for qq in range(4):
        at = slice(qq * LANE_TILES, (qq + 1) * LANE_TILES)
        column_sum = sums_ref[GATHERED + qq * 16 : GATHERED + qq * 16 + LANE_TILES, :]
        new_col = beta_two * col_factor_ref[at, :] + (1.0 - beta_two) * (
            (column_sum + col_rest_ref[at, :]) / FULL_ROWS
        )
        new_col_ref[at, :] = new_col
        inverse_col = lax.rsqrt(new_col)
        for lb in range(LANE_TILES):
            b = (qq * LANE_TILES + lb) * 128
            g = sums_ref[pl.ds(qq * SPREAD + lb, 3, stride=LANE_TILES), :]
            change = g * row_scale * inverse_col[lb : lb + 1, :]
            new_momentum = beta_one * momentum_ref[:, b : b + 128] + change
            new_momentum_ref[:, b : b + 128] = new_momentum
            new_matrix_ref[:, b : b + 128] = matrix_ref[:, b : b + 128] - new_momentum


def place_kernel(
    matrix_ref, momentum_ref, row_ref, col_ref, new_matrix_ref, new_momentum_ref, new_row_ref, new_col_ref, sem
):
    copies = []
    for n, (src, dst) in enumerate(
        ((matrix_ref, new_matrix_ref), (momentum_ref, new_momentum_ref), (col_ref, new_col_ref))
    ):
        copy = pltpu.make_async_copy(src, dst, sem.at[n])
        copy.start()
        copies.append(copy)
    for j in range(3):
        new_row_ref[j] = row_ref[j : j + 1, 0:1][0, 0]
    for copy in copies:
        copy.wait()


def on_device(inputs, cotangent, matrix, momentum, row_factor, col_factor, row_rest, col_rest):
    vmem = pl.BlockSpec(memory_space=VMEM)
    smem = pl.BlockSpec(memory_space=pltpu.SMEM)
    hbm = pl.BlockSpec(memory_space=pltpu.HBM)
    dma = pltpu.SemaphoreType.DMA
    held = pltpu.with_memory_space_constraint
    done = pl.pallas_call(
        reduce_kernel,
        out_shape=(
            jax.ShapeDtypeStruct(matrix.shape, F32),
            jax.ShapeDtypeStruct(matrix.shape, F32),
            jax.ShapeDtypeStruct((8, 128), F32),
            jax.ShapeDtypeStruct((36, 128), F32),
        ),
        in_specs=[hbm] * 8,
        out_specs=(vmem,) * 4,
        scratch_shapes=[
            VMEM((ROWS, 480), jnp.bfloat16),
            VMEM((3, 4608), F32),
            pltpu.SMEM((3,), F32),
            pltpu.SMEM((3,), F32),
            VMEM((3, 4608), F32),
            VMEM((36, 128), F32),
            VMEM((36, 128), F32),
            VMEM((SUMS + 8, 128), F32),
            VMEM((ROWS, 480), jnp.bfloat16),
            VMEM((4, 480, GROUP), jnp.bfloat16),
            VMEM((2, 8, 2, A_ROWS, 128), F32),
            VMEM((8, 2, A_ROWS, 128), F32),
            VMEM((2, 4, 2, 2, B_ROWS, 128), F32),
            VMEM((4, 2, 2, B_ROWS, 128), F32),
            VMEM((16, A_ROWS, 128), F32),
            VMEM((4, A_ROWS, 128), F32),
            VMEM((4, 4, 2, B_ROWS, 128), F32),
            VMEM((8, B_ROWS, 128), F32),
            VMEM((9 * SPREAD, 128), F32),
            VMEM((4, SPREAD, 128), F32),
            VMEM((8, 128), F32),
            VMEM((8, 128), F32),
            VMEM((16, 128), F32),
            VMEM((272, 128), F32),
            VMEM((16, 128), F32),
            VMEM((8, 16, 128), F32),
            dma, dma((6,)), dma((4,)),
            dma, dma((8,)), dma, dma((4,)), dma, dma, dma, dma((2, 2, 4)),
            dma((2,)), dma, dma((2,)), dma, dma, dma, dma, dma, dma, dma, dma, dma, dma, dma,
        ],
        compiler_params=pltpu.CompilerParams(
            collective_id=0, has_side_effects=True, vmem_limit_bytes=40 * 1024 * 1024
        ),
        name="reduce",
    )(
        *[
            held(v, pltpu.HBM)
            for v in (
                inputs.T, cotangent, matrix, row_factor, row_rest, momentum,
                col_factor.reshape(36, 128), col_rest.reshape(36, 128),
            )
        ]
    )
    new_matrix, new_momentum, new_row, new_col = pl.pallas_call(
        place_kernel,
        out_shape=(
            jax.ShapeDtypeStruct(matrix.shape, F32),
            jax.ShapeDtypeStruct(matrix.shape, F32),
            jax.ShapeDtypeStruct((3,), F32),
            jax.ShapeDtypeStruct((36, 128), F32),
        ),
        in_specs=[vmem] * 4,
        out_specs=(hbm, hbm, smem, hbm),
        scratch_shapes=[dma((3,))],
        name="place",
    )(*[held(v, VMEM) for v in done])
    return (new_matrix, new_momentum, new_row, new_col.reshape(4608))


def solution(mesh):
    placed = (
        P("dp", None),
        P("dp", "mp"),
        P("dp", "mp"),
        P("dp", "mp"),
        P("dp"),
        P("mp"),
        P("dp"),
        P("mp"),
    )
    return jax.shard_map(
        on_device,
        mesh=mesh,
        in_specs=placed,
        out_specs=(P("dp", "mp"), P("dp", "mp"), P("dp"), P("mp")),
        check_vma=False,
    )
```
